32 devices in a mesh: member: 2 (over y), lon: 8 (over z, x), lat: 2 (over core).
Axes of the slice: x: 2, y: 2, z: 4, core: 2. Of those that a mesh axis runs over, the one named last changes fastest.
Arguments:
- innovation: float32 [65536], P(('member', 'lon', 'lat')), parts along dimension 0, may hold values from -6 to 6
- fractions: float32 [3, 65536], P(None, ('member', 'lon', 'lat')), parts along dimension 1, may hold values from 0 to 1
- owner: int32 [65536, 1], P(('member', 'lon', 'lat')), parts along dimension 0, may hold values from 0 to 15; in each aligned block of 2048 rows (0 to 2047, 2048 to 4095, ...) at most 256 rows name the same one
- obs_row: int32 [65536], P(('member', 'lon', 'lat')), parts along dimension 0, may hold values from 0 to 14
- obs_col: int32 [65536], P(('member', 'lon', 'lat')), parts along dimension 0, may hold values from 0 to 254
- obs_field: int32 [65536], P(('member', 'lon', 'lat')), parts along dimension 0, may hold values from 0 to 3
- obs_level: int32 [65536], P(('member', 'lon', 'lat')), parts along dimension 0, may hold values from 0 to 30
- land_mask: int32 [32, 2048], P('lat', 'lon'), may hold values 0 or 1
- kappa: float32 [32, 2048], P('lat', 'lon'), may hold values from 1 to 20
- sigma: float32 [128, 32, 2048], P(None, 'lat', 'lon'), may hold values from 0.5 to 2
- balance: float32 [128, 128], replicated, may hold values from -0.5 to 0.5
Outputs:
- gradient: float32 [256, 32, 2048], P('member', 'lat', 'lon'), parts along dimension 0
The draws below stay inside these ranges and needn't reach their ends.
There are 2 independent parts, one for each index of `member`. The reference program is written for one: setup_inputs(seed, part) draws one part's arguments, and reference() takes and returns one part's arrays. A program takes and returns all parts, laid end to end along the dimension named above; an argument that names none is the same for every part. Nothing has to cross between parts.
Inputs may be any that keep to these rules, and one draw needn't show every extreme that they name: Within each device's block of 2048 innovations no tile is owner more than 256 times, and some tile is owner exactly 256 times.
All inputs are finite; a program needn't handle non-finite values. No bound on the sum of `land_mask` on one device may be relied on, other than what follows from the above.
Results may differ from the reference program's by a relative error of at most 0.0003.
Values sent between devices are 32-bit elements; how exact they have to be, the bound alone decides.
A program may use at most 64 MiB of HBM per device.

```python
import math
import jax
import jax.numpy as jnp
import numpy as np
from jax import lax

FIELDS = 4
LEV = 32
TY = 16
TX = 256
OBS_DEV = 2048
C = 128
TILES = 16
CAP = 256
NY = 32
NX = 2048
OBS = 32768
N_LAT = 2


def place_ends(drawn, rng, low, largest):
    index_at = [jax.random.randint(jax.random.fold_in(rng, axis), (), 0, length) for axis, length in enumerate(drawn.shape)]
    main_axis = drawn.shape.index(max(drawn.shape))
    beside = index_at[:main_axis] + [(index_at[main_axis] + 1) % drawn.shape[main_axis]] + index_at[main_axis + 1:]
    return drawn.at[tuple(index_at)].set(low).at[tuple(beside)].set(largest)


def level_of(stream_key, extent, pieces, smallest, top_value):
    def one(position, parts):
        steps = jax.random.uniform(jax.random.fold_in(jax.random.fold_in(stream_key, 6), position), (parts,), jnp.float32, smallest / len(pieces), top_value / len(pieces))
        return jnp.repeat(jnp.exp(steps), extent[position] // parts).reshape((-1,) + (1,) * (len(extent) - position - 1))

    loudness = one(*pieces[0])
    for cut in pieces[1:]:
        loudness = loudness * one(*cut)
    return loudness


def deal_out(stream_key, own, number, rows, count, top, limit, skew):
    sequence = jax.random.permutation(stream_key, count)
    packed, ordinary = shares(count, rows * top, limit, skew, True), shares(count, rows * top, limit, skew, False)
    places = jnp.arange(count)

    def named(lengths, turn):
        used = int((lengths > 0).sum())
        fixed = max(1, used // 4)
        shifted = fixed + (places - fixed + turn * (used - fixed)) % max(1, count - fixed)
        return jnp.zeros((count,), jnp.int32).at[sequence[jnp.where(places < fixed, places, shifted)]].set(jnp.asarray(lengths, jnp.int32))

    lengths = jnp.where(number % 4 == 0, named(packed, number // 4), named(ordinary, number - number // 4 - 1))
    mixed = jax.random.permutation(jax.random.fold_in(own, 3), count)
    giver, receiver = mixed[0:count // 2 * 2:2], mixed[1:count // 2 * 2:2]
    slack = jnp.minimum(lengths[giver] - 1, limit - lengths[receiver]) // 2
    slack = jnp.where((giver == sequence[0]) | (receiver == sequence[0]) | (lengths[receiver] == 0), 0, jnp.maximum(slack, 0))
    shifted = jax.random.randint(jax.random.fold_in(own, 4), (count // 2,), 0, 1 << 20) % (slack + 1)
    lengths = lengths.at[giver].add(-shifted).at[receiver].add(shifted)
    items = jnp.searchsorted(jnp.cumsum(lengths), jnp.arange(rows * top), side="right").astype(jnp.int32)
    grid = items.reshape(top, rows).T
    grid = grid[jax.random.permutation(jax.random.fold_in(own, 1), rows)]
    turn = jax.random.randint(jax.random.fold_in(own, 2), (rows, 1), 0, top)
    return jnp.take_along_axis(grid, (jnp.arange(top)[None, :] + turn) % top, axis=1)


def shares(number_of, total, bound, skew, full):
    loads = [(1 << 20) // math.isqrt(grade ** skew) + 1 for grade in range(1, number_of + 1)]
    largest = bound if full else min(bound, max(-(-total // number_of), total * loads[0] // sum(loads)))
    least = 1 if total - largest >= number_of - 1 else 0
    counts, surplus = [largest] + [least] * (number_of - 1), total - largest - least * (number_of - 1)
    while surplus > 0:
        free = [i for i in range(1, number_of) if counts[i] < largest] or [i for i in range(1, number_of) if counts[i] < bound]
        pool, left = sum([loads[i] for i in free]), surplus
        for i in free:
            more = min(bound - counts[i], max(1, left * loads[i] // pool), surplus)
            counts[i] = counts[i] + more
            surplus = surplus - more
    return np.array(counts)


def bell_draw(rng, dims, deviation, bound, cuts=(), kind=jnp.bfloat16):
    result = jax.random.normal(rng, dims, jnp.float32) * deviation
    if len(cuts) > 0:
        result = level_of(rng, dims, cuts, -0.22, 0.18) * result
    return jnp.clip(result, min=-bound, max=bound).astype(kind)


def setup_inputs(seed: int = 0, part: int = 0) -> dict:
    splits = jax.random.split(jax.random.key(seed), 12)
    part_keys = jax.random.split(jax.random.fold_in(splits[11], part), 12)
    innovation = bell_draw(part_keys[0], (OBS,), 1.0, 6.0, ((0, 16),), jnp.float32)
    fractions = jnp.clip(1.0 * jax.random.uniform(part_keys[1], (3, OBS), jnp.float32) ** level_of(part_keys[1], (3, OBS), ((1, 16),), -0.2, 0.2), 0.0, 1.0)
    owner_keys = jax.random.split(jax.random.fold_in(part_keys[2], 1), OBS // OBS_DEV)
    owner_turns = jax.random.permutation(jax.random.fold_in(part_keys[2], 3), OBS // OBS_DEV)
    owner = jax.vmap(lambda own, number: deal_out(jax.random.fold_in(part_keys[2], 2), own, number, OBS_DEV, TILES, 1, CAP, 2))(owner_keys, owner_turns).reshape((OBS, 1))
    obs_row = place_ends(jax.random.randint(part_keys[3], (OBS,), 0, TY - 1), jax.random.fold_in(part_keys[3], 1), 0, (TY - 1) - 1).astype(jnp.int32)
    obs_col = place_ends(jax.random.randint(part_keys[4], (OBS,), 0, TX - 1), jax.random.fold_in(part_keys[4], 1), 0, (TX - 1) - 1).astype(jnp.int32)
    obs_field = place_ends(jax.random.randint(part_keys[5], (OBS,), 0, FIELDS), jax.random.fold_in(part_keys[5], 1), 0, FIELDS - 1).astype(jnp.int32)
    obs_level = place_ends(jax.random.randint(part_keys[6], (OBS,), 0, LEV - 1), jax.random.fold_in(part_keys[6], 1), 0, (LEV - 1) - 1).astype(jnp.int32)
    land_mask = place_ends((jax.random.randint(splits[7], (NY, NX), 0, 5) < 4).astype(jnp.int32), jax.random.fold_in(splits[7], 1), 0, 1)
    kappa = jnp.clip(jnp.exp(math.log(20.0) - 2.9957323 * jax.random.uniform(splits[8], (NY, NX), jnp.float32) ** level_of(splits[8], (NY, NX), ((0, 2), (1, 8)), -0.2, 0.2)), 1.0, 20.0)
    sigma = jnp.clip(jnp.exp(math.log(2.0) - 1.3862944 * jax.random.uniform(splits[9], (C, NY, NX), jnp.float32) ** level_of(splits[9], (C, NY, NX), ((1, 2), (2, 8)), -0.2, 0.2)), 0.5, 2.0)
    balance = bell_draw(splits[10], (C, C), C ** -0.5, 0.5, (), jnp.float32)
    return dict(innovation=innovation, fractions=fractions, owner=owner, obs_row=obs_row, obs_col=obs_col, obs_field=obs_field, obs_level=obs_level, land_mask=land_mask, kappa=kappa, sigma=sigma, balance=balance)


def corner_terms(values, fractions):
    fy = fractions[0]
    fx = fractions[1]
    fz = fractions[2]
    terms = []
    for lz in (0, 1):
        wz = fz if lz else 1.0 - fz
        for dy in (0, 1):
            wy = fy if dy else 1.0 - fy
            for dx in (0, 1):
                wx = fx if dx else 1.0 - fx
                terms.append(values * (wz * wy * wx))
    return jnp.stack(terms)


def corner_offsets(cells, stride):
    return jnp.array([lz * cells + dy * stride + dx for lz in (0, 1) for dy in (0, 1) for dx in (0, 1)], dtype=jnp.int32)


def face_coefficients(ext):
    kval = ext[0]
    mval = ext[1]
    kc = kval[1:-1, 1:-1]
    mc = mval[1:-1, 1:-1]
    south = 0.5 * (kc + kval[:-2, 1:-1]) * mc * mval[:-2, 1:-1]
    north = 0.5 * (kc + kval[2:, 1:-1]) * mc * mval[2:, 1:-1]
    west = 0.5 * (kc + kval[1:-1, :-2]) * mc * mval[1:-1, :-2]
    east = 0.5 * (kc + kval[1:-1, 2:]) * mc * mval[1:-1, 2:]
    denom = 1.0 + south + north + west + east
    return south, north, west, east, denom


def relax(u_ext, source, coefs):
    south, north, west, east, denom = coefs
    total = source + south * u_ext[:, :-2, 1:-1] + north * u_ext[:, 2:, 1:-1]
    total = total + west * u_ext[:, 1:-1, :-2] + east * u_ext[:, 1:-1, 2:]
    return total / denom


def reference(innovation, fractions, owner, obs_row, obs_col, obs_field, obs_level, land_mask, kappa, sigma, balance):
    dest = owner[:, 0]
    grid_row = (dest % N_LAT) * TY + obs_row
    grid_col = (dest // N_LAT) * TX + obs_col
    channel = obs_field * LEV + obs_level
    cells = NY * NX
    base = channel * cells + grid_row * NX + grid_col
    terms = corner_terms(innovation, fractions)
    index = (base[None, :] + corner_offsets(cells, NX)[:, None]).astype(jnp.int32)
    maskf = land_mask.astype(jnp.float32)
    forcing = jnp.zeros((C * cells,), jnp.float32).at[index.reshape(-1)].add(terms.reshape(-1))
    forcing = forcing.reshape(C, NY, NX) * maskf
    scaled = sigma * forcing
    balanced = jnp.dot(balance.T, scaled.reshape(C, cells), precision=lax.Precision.HIGHEST,
                       preferred_element_type=jnp.float32).reshape(C, NY, NX)
    stacked = jnp.pad(jnp.stack([kappa * maskf, maskf]), ((0, 0), (1, 1), (1, 1)))
    coefs = face_coefficients(stacked)

    def diffuse(block):
        u = block / coefs[4]
        for sweep in range(3):
            u = relax(jnp.pad(u, ((0, 0), (1, 1), (1, 1))), block, coefs)
        return u

    groups = balanced.reshape(C // 2, 2, NY, NX)
    return lax.map(diffuse, groups).reshape(C, NY, NX)
```

```python
import functools
import math

import jax
import jax.numpy as jnp
from jax import lax
from jax.experimental import pallas as pl
from jax.experimental.pallas import tpu as pltpu
from jax.sharding import PartitionSpec as P

LEV = 32
MESH = pl.DeviceIdType.MESH
NT = (((1,), (1,)), ((), ()))
LANES = 128


def iota_f(shape, dim):
    return lax.broadcasted_iota(jnp.int32, shape, dim).astype(jnp.float32)


def hat(ids, low, first, second):
    return jnp.where(ids == low, first, 0.0) + jnp.where(ids == low + 1.0, second, 0.0)


def split2(x):
    hi = x.astype(jnp.bfloat16)
    return hi, (x - hi.astype(jnp.float32)).astype(jnp.bfloat16)


def buckets(innov, frac, owner, orow, ocol, ofield, olev, tiles, slots):
    obs = innov.shape[1]
    blk = math.gcd(obs, 256)
    dest = owner[...]
    hot = jnp.where(lax.broadcasted_iota(jnp.int32, (tiles, obs), 0) == dest, 1.0, 0.0)
    before = jnp.where(iota_f((blk, blk), 0) < iota_f((blk, blk), 1), 1.0, 0.0).astype(jnp.bfloat16)
    carry = jnp.zeros((tiles, 1), jnp.float32)
    ranks = []
    for b in range(obs // blk):
        part = hot[:, b * blk : (b + 1) * blk]
        ahead = jnp.dot(part.astype(jnp.bfloat16), before, preferred_element_type=jnp.float32) + carry
        ranks.append(jnp.sum(ahead * part, axis=0, keepdims=True))
        carry = carry + jnp.sum(part, axis=1, keepdims=True)
    rank = jnp.concatenate(ranks, axis=1)
    slot_hot = jnp.where(iota_f((slots, obs), 0) == rank, 1.0, 0.0).astype(jnp.bfloat16)
    channel = ofield[...] * LEV + olev[...]
    ints = [channel.astype(jnp.float32), orow[...].astype(jnp.float32), ocol[...].astype(jnp.float32)]
    rest = jnp.concatenate(
        [innov[...], frac[...]] + ints + [jnp.zeros((1, obs), jnp.float32)], axis=0
    )
    mine = lax.broadcasted_iota(jnp.int32, (tiles, 8, obs), 0) == dest[None]
    placed = jnp.zeros((tiles * 8, slots), jnp.float32)
    for piece in range(3):
        top = rest.astype(jnp.bfloat16).astype(jnp.float32)
        rest = rest - top
        spread = jnp.where(mine, top[None], 0.0).reshape(tiles * 8, obs).astype(jnp.bfloat16)
        placed = placed + lax.dot_general(spread, slot_hot, NT, preferred_element_type=jnp.float32)
    return placed.reshape(tiles, 8, slots)


def kernel(
    n_lon,
    n_lat,
    innov,
    frac,
    owner,
    orow,
    ocol,
    ofield,
    olev,
    mask,
    kappa,
    balance,
    sigma,
    out,
    sig,
    send,
    recv,
    km,
    km_in,
    coef,
    a_ref,
    b_ref,
    r_hi,
    r_lo,
    acc,
    u,
    edge_out,
    edge_in,
    edge_t,
    packs,
    sig_sem,
    send_sem,
    recv_sem,
    km_send,
    km_recv,
    halo_send,
    halo_recv,
):
    tiles = n_lon * n_lat
    rows, cols = mask.shape
    chans = balance.shape[0]
    slots = recv.shape[2]
    halves = cols // LANES
    lon = lax.axis_index("lon")
    lat = lax.axis_index("lat")
    me = lon * n_lat + lat

    def where_is(tile):
        return {"lon": tile // n_lat, "lat": lax.rem(tile, n_lat)}

    sig_copy = pltpu.make_async_copy(sigma, sig, sig_sem)
    sig_copy.start()
    barrier = pltpu.get_barrier_semaphore()

    @pl.loop(1, tiles)
    def _(k):
        pl.semaphore_signal(
            barrier, inc=1, device_id=where_is(lax.rem(me + k, tiles)), device_id_type=MESH
        )

    maskf = mask[...].astype(jnp.float32)
    km[0] = kappa[...] * maskf
    km[1] = maskf
    send[...] = buckets(innov, frac, owner, orow, ocol, ofield, olev, tiles, slots)
    pl.semaphore_wait(barrier, tiles - 1)

    def item_copy(target, origin):
        return pltpu.make_async_remote_copy(
            src_ref=send.at[target],
            dst_ref=recv.at[origin],
            send_sem=send_sem.at[target],
            recv_sem=recv_sem.at[origin],
            device_id=where_is(target),
            device_id_type=MESH,
        )

    @pl.loop(1, tiles)
    def _(k):
        item_copy(lax.rem(me + k, tiles), me).start()

    has = (lat > 0, lat < n_lat - 1, lon > 0, lon < n_lon - 1)
    there = (
        {"lat": lat - 1},
        {"lat": lat + 1},
        {"lon": lon - 1},
        {"lon": lon + 1},
    )
    opposite = (1, 0, 3, 2)

    def km_copy(side):
        return pltpu.make_async_remote_copy(
            src_ref=km,
            dst_ref=km_in.at[opposite[side]],
            send_sem=km_send.at[side],
            recv_sem=km_recv.at[opposite[side]],
            device_id=there[side],
            device_id_type=MESH,
        )

    def km_arrival(side):
        return pltpu.make_async_remote_copy(
            src_ref=km,
            dst_ref=km_in.at[side],
            send_sem=km_send.at[side],
            recv_sem=km_recv.at[side],
            device_id=there[side],
            device_id_type=MESH,
        )

    for side in range(4):

        @pl.when(has[side])
        def _():
            km_copy(side).start()

        @pl.when(jnp.logical_not(has[side]))
        def _():
            km_in[side] = jnp.zeros((2, rows, cols), jnp.float32)

    recv[me] = send[me]
    acc[...] = jnp.zeros(acc.shape, jnp.float32)
    group = a_ref.shape[1] // slots
    step_rows = math.gcd(rows, 4)

    @pl.loop(0, tiles // group)
    def _(chunk):
        pieces = []
        for i in range(group):
            k = chunk * group + i
            origin = lax.rem(me + tiles - k, tiles)

            @pl.when(k > 0)
            def _():
                item_copy(origin, origin).wait_recv()

            pieces.append(recv[origin])
        items = pieces[0] if group == 1 else jnp.concatenate(pieces, axis=1)
        depth = items.shape[1]
        val, fy, fx, fz = items[0:1], items[1:2], items[2:3], items[3:4]
        ch, row, col = items[4:5], items[5:6], items[6:7]
        a_ref[...] = hat(iota_f((chans, depth), 0), ch, val * (1.0 - fz), val * fz)
        b_ref[...] = hat(iota_f((rows, depth), 0), row, 1.0 - fy, fy)
        hi, lo = split2(hat(iota_f((cols, depth), 0), col, 1.0 - fx, fx))
        r_hi[...] = hi
        r_lo[...] = lo

        @pl.loop(0, rows // step_rows)
        def _(part):
            lefts = [
                a_ref[...] * b_ref[pl.ds(part * step_rows + j, 1), :] for j in range(step_rows)
            ]
            left_hi, left_lo = split2(jnp.concatenate(lefts, axis=0))
            dot = functools.partial(
                lax.dot_general, dimension_numbers=NT, preferred_element_type=jnp.float32
            )
            total = dot(left_hi, r_hi[...]) + dot(left_lo, r_hi[...]) + dot(left_hi, r_lo[...])
            here = pl.ds(pl.multiple_of(part * step_rows, step_rows), step_rows)
            acc[here] += total.reshape(step_rows, chans, cols)

    for side in range(4):

        @pl.when(has[side])
        def _():
            km_arrival(side).wait_recv()
            km_copy(side).wait_send()

    kc, mc = km[0], km[1]

    def beside(plane):
        mid = km[plane]
        south = jnp.concatenate([km_in[0, plane][rows - 1 :], mid[: rows - 1]], axis=0)
        north = jnp.concatenate([mid[1:], km_in[1, plane][:1]], axis=0)
        west = jnp.concatenate([km_in[2, plane][:, cols - 1 :], mid[:, : cols - 1]], axis=1)
        east = jnp.concatenate([mid[:, 1:], km_in[3, plane][:, :1]], axis=1)
        return (south, north, west, east)

    faces = [0.5 * (kc + kn) * mc * mn for kn, mn in zip(beside(0), beside(1))]
    inv = 1.0 / (1.0 + faces[0] + faces[1] + faces[2] + faces[3])
    for side in range(4):
        coef[side] = faces[side] * inv
    coef[4] = inv
    coef[5] = mc

    lane = lax.broadcasted_iota(jnp.int32, (chans, LANES), 1)

    def pack(r, first, last):
        packs[0] = jnp.where(lane == r, pltpu.roll(first, r, 1), packs[0])
        packs[1] = jnp.where(lane == r, pltpu.roll(last, r + 1, 1), packs[1])

    def halo(sweep, side, arriving):
        slot = opposite[side] if not arriving else side
        if side < 2:
            src = u.at[sweep, 1 if side == 0 else rows]
            dst = u.at[sweep, 0 if slot == 0 else rows + 1]
        else:
            src = edge_out.at[sweep, side - 2]
            dst = edge_in.at[sweep, slot - 2]
        return pltpu.make_async_remote_copy(
            src_ref=src,
            dst_ref=dst,
            send_sem=halo_send.at[sweep, side],
            recv_sem=halo_recv.at[sweep, slot],
            device_id=there[side],
            device_id_type=MESH,
        )

    def exchange(sweep):
        for j in range(2):
            edge_out[sweep, j] = jnp.transpose(packs[j])[:rows]
        for side in (2, 3, 0, 1):

            @pl.when(has[side])
            def _():
                halo(sweep, side, False).start()

        for side in range(4):

            @pl.when(jnp.logical_not(has[side]))
            def _():
                if side < 2:
                    u[sweep, 0 if side == 0 else rows + 1] = jnp.zeros((chans, cols), jnp.float32)
                else:
                    edge_in[sweep, side - 2] = jnp.zeros((rows, chans), jnp.float32)

            @pl.when(has[side])
            def _():
                halo(sweep, side, True).wait_recv()
                halo(sweep, side, False).wait_send()

        for j in range(2):
            filled = jnp.concatenate(
                [edge_in[sweep, j], jnp.zeros((LANES - rows, chans), jnp.float32)], axis=0
            )
            edge_t[j] = jnp.transpose(filled)

    packs[...] = jnp.zeros(packs.shape, jnp.float32)
    sig_copy.wait()
    bal_t = jnp.transpose(balance[...])

    @pl.loop(0, rows)
    def _(r):
        scale = jnp.concatenate(
            [sig[h, pl.ds(r, chans, stride=rows), :] for h in range(halves)], axis=1
        )
        scaled = acc[r] * coef[5, pl.ds(r, 1), :] * scale
        balanced = jnp.dot(
            bal_t, scaled, precision=lax.Precision.HIGHEST, preferred_element_type=jnp.float32
        )
        start = balanced * coef[4, pl.ds(r, 1), :]
        acc[r] = start
        u[0, r + 1] = start
        pack(r, start[:, :LANES], start[:, cols - LANES :])

    for sweep in range(3):
        exchange(sweep)

        @pl.loop(0, rows)
        def _(r):
            mid = u[sweep, r + 1]
            parts = [mid[:, h * LANES : (h + 1) * LANES] for h in range(halves)]
            up = [pltpu.roll(p, 1, 1) for p in parts]
            down = [pltpu.roll(p, LANES - 1, 1) for p in parts]
            before = pltpu.roll(edge_t[0], lax.rem(LANES - r, LANES), 1)
            after = pltpu.roll(edge_t[1], LANES - 1 - r, 1)
            west = [jnp.where(lane == 0, q, p) for p, q in zip(up, [before] + up[:-1])]
            east = [jnp.where(lane == LANES - 1, q, p) for p, q in zip(down, down[1:] + [after])]
            west = jnp.concatenate(west, axis=1)
            east = jnp.concatenate(east, axis=1)
            total = acc[r] + coef[0, pl.ds(r, 1), :] * u[sweep, r]
            total = total + coef[1, pl.ds(r, 1), :] * u[sweep, r + 2]
            total = total + coef[2, pl.ds(r, 1), :] * west
            total = total + coef[3, pl.ds(r, 1), :] * east
            if sweep < 2:
                u[sweep + 1, r + 1] = total
                pack(r, total[:, :LANES], total[:, cols - LANES :])
            else:
                out[r] = total

    @pl.loop(1, tiles)
    def _(k):
        item_copy(lax.rem(me + k, tiles), me).wait_send()


def on_device(
    innovation,
    fractions,
    owner,
    obs_row,
    obs_col,
    obs_field,
    obs_level,
    land_mask,
    kappa,
    sigma,
    balance,
):
    n_lon = lax.axis_size("lon")
    n_lat = lax.axis_size("lat")
    tiles = n_lon * n_lat
    obs = innovation.shape[0]
    slots = 2 * obs // tiles
    chans, rows, cols = sigma.shape
    halves = cols // LANES
    depth = min(1024, tiles * slots)
    line = lambda x: x.reshape(1, obs)
    vmem = pl.BlockSpec(memory_space=pltpu.VMEM)
    f32 = jnp.float32
    sig_lines = jnp.transpose(sigma.reshape(chans * rows, halves, LANES), (1, 0, 2))
    field = pl.pallas_call(
        functools.partial(kernel, n_lon, n_lat),
        out_shape=jax.ShapeDtypeStruct((rows, chans, cols), f32),
        in_specs=[vmem] * 10 + [pl.BlockSpec(memory_space=pl.ANY)],
        out_specs=vmem,
        scratch_shapes=[
            pltpu.VMEM((halves, chans * rows, LANES), f32),
            pltpu.VMEM((tiles, 8, slots), f32),
            pltpu.VMEM((tiles, 8, slots), f32),
            pltpu.VMEM((2, rows, cols), f32),
            pltpu.VMEM((4, 2, rows, cols), f32),
            pltpu.VMEM((6, rows, cols), f32),
            pltpu.VMEM((chans, depth), f32),
            pltpu.VMEM((rows, depth), f32),
            pltpu.VMEM((cols, depth), jnp.bfloat16),
            pltpu.VMEM((cols, depth), jnp.bfloat16),
            pltpu.VMEM((rows, chans, cols), f32),
            pltpu.VMEM((3, rows + 2, chans, cols), f32),
            pltpu.VMEM((3, 2, rows, chans), f32),
            pltpu.VMEM((3, 2, rows, chans), f32),
            pltpu.VMEM((2, chans, LANES), f32),
            pltpu.VMEM((2, chans, LANES), f32),
            pltpu.SemaphoreType.DMA,
            pltpu.SemaphoreType.DMA((tiles,)),
            pltpu.SemaphoreType.DMA((tiles,)),
            pltpu.SemaphoreType.DMA((4,)),
            pltpu.SemaphoreType.DMA((4,)),
            pltpu.SemaphoreType.DMA((3, 4)),
            pltpu.SemaphoreType.DMA((3, 4)),
        ],
        compiler_params=pltpu.CompilerParams(
            collective_id=0, has_side_effects=True, vmem_limit_bytes=56 * 1024 * 1024
        ),
    )(
        line(innovation),
        fractions,
        line(owner),
        line(obs_row),
        line(obs_col),
        line(obs_field),
        line(obs_level),
        land_mask,
        kappa,
        balance,
        sig_lines,
    )
    return jnp.transpose(field, (1, 0, 2))


def solution(mesh):
    spread = P(("member", "lon", "lat"))
    in_specs = (
        spread,
        P(None, ("member", "lon", "lat")),
        P(("member", "lon", "lat"), None),
        spread,
        spread,
        spread,
        spread,
        P("lat", "lon"),
        P("lat", "lon"),
        P(None, "lat", "lon"),
        P(),
    )
    out_specs = P("member", "lat", "lon")
    return jax.shard_map(
        on_device, mesh=mesh, in_specs=in_specs, out_specs=out_specs, check_vma=False
    )
```

```python
import functools
import math

import jax
import jax.numpy as jnp
from jax import lax
from jax.experimental import pallas as pl
from jax.experimental.pallas import tpu as pltpu
from jax.sharding import PartitionSpec as P

LEV = 32
MESH = pl.DeviceIdType.MESH
NT = (((1,), (1,)), ((), ()))
LANES = 128
BAND = 8


def iota_f(shape, dim):
    return lax.broadcasted_iota(jnp.int32, shape, dim).astype(jnp.float32)


def hat(ids, low, first, second):
    return jnp.where(ids == low, first, 0.0) + jnp.where(ids == low + 1.0, second, 0.0)


def split2(x):
    hi = x.astype(jnp.bfloat16)
    return hi, (x - hi.astype(jnp.float32)).astype(jnp.bfloat16)


def turn(x, shift):
    shift = shift % LANES
    return pltpu.roll(x, shift, 1) if shift else x


def pack(lane, r, source, held, values):
    return jnp.where(lane == r, turn(values, r - source), held)


def buckets(innov, frac, owner, orow, ocol, ofield, olev, tiles, slots):
    obs = innov.shape[1]
    blk = math.gcd(obs, 256)
    dest = owner[...]
    hot = jnp.where(lax.broadcasted_iota(jnp.int32, (tiles, obs), 0) == dest, 1.0, 0.0)
    before = jnp.where(iota_f((blk, blk), 0) < iota_f((blk, blk), 1), 1.0, 0.0).astype(jnp.bfloat16)
    carry = jnp.zeros((tiles, 1), jnp.float32)
    ranks = []
    for b in range(obs // blk):
        part = hot[:, b * blk : (b + 1) * blk]
        ahead = jnp.dot(part.astype(jnp.bfloat16), before, preferred_element_type=jnp.float32) + carry
        ranks.append(jnp.sum(ahead * part, axis=0, keepdims=True))
        carry = carry + jnp.sum(part, axis=1, keepdims=True)
    rank = jnp.concatenate(ranks, axis=1)
    slot_hot = jnp.where(iota_f((slots, obs), 0) == rank, 1.0, 0.0).astype(jnp.bfloat16)
    channel = ofield[...] * LEV + olev[...]
    ints = [channel.astype(jnp.float32), orow[...].astype(jnp.float32), ocol[...].astype(jnp.float32)]
    rest = jnp.concatenate(
        [innov[...], frac[...]] + ints + [jnp.zeros((1, obs), jnp.float32)], axis=0
    )
    mine = lax.broadcasted_iota(jnp.int32, (tiles, 8, obs), 0) == dest[None]
    placed = jnp.zeros((tiles * 8, slots), jnp.float32)
    for piece in range(3):
        top = rest.astype(jnp.bfloat16).astype(jnp.float32)
        rest = rest - top
        spread = jnp.where(mine, top[None], 0.0).reshape(tiles * 8, obs).astype(jnp.bfloat16)
        placed = placed + lax.dot_general(spread, slot_hot, NT, preferred_element_type=jnp.float32)
    return placed.reshape(tiles, 8, slots)


def kernel(
    n_lon,
    n_lat,
    innov,
    frac,
    owner,
    orow,
    ocol,
    ofield,
    olev,
    mask,
    kappa,
    balance,
    sigma,
    out,
    sig,
    send,
    recv,
    km,
    km_in,
    coef,
    a_ref,
    b_ref,
    r_hi,
    r_lo,
    acc,
    u,
    edge_out,
    edge_in,
    edge_t,
    packs,
    sig_sem,
    send_sem,
    recv_sem,
    km_send,
    km_recv,
    halo_send,
    halo_recv,
):
    tiles = n_lon * n_lat
    rows, cols = mask.shape
    chans = balance.shape[0]
    slots = recv.shape[2]
    halves = cols // LANES
    lon = lax.axis_index("lon")
    lat = lax.axis_index("lat")
    me = lon * n_lat + lat

    def where_is(tile):
        return {"lon": tile // n_lat, "lat": lax.rem(tile, n_lat)}

    sig_copies = [
        pltpu.make_async_copy(sigma.at[:, pl.ds(h * LANES, LANES)], sig.at[h], sig_sem.at[h])
        for h in range(halves)
    ]
    for copy in sig_copies:
        copy.start()
    barrier = pltpu.get_barrier_semaphore()

    @pl.loop(1, tiles)
    def _(k):
        pl.semaphore_signal(
            barrier, inc=1, device_id=where_is(lax.rem(me + k, tiles)), device_id_type=MESH
        )

    maskf = mask[...].astype(jnp.float32)
    km[0] = kappa[...] * maskf
    km[1] = maskf
    send[...] = buckets(innov, frac, owner, orow, ocol, ofield, olev, tiles, slots)
    pl.semaphore_wait(barrier, tiles - 1)

    def item_copy(target, origin):
        return pltpu.make_async_remote_copy(
            src_ref=send.at[target],
            dst_ref=recv.at[origin],
            send_sem=send_sem.at[target],
            recv_sem=recv_sem.at[origin],
            device_id=where_is(target),
            device_id_type=MESH,
        )

    @pl.loop(1, tiles)
    def _(k):
        item_copy(lax.rem(me + k, tiles), me).start()

    has = (lat > 0, lat < n_lat - 1, lon > 0, lon < n_lon - 1)
    there = (
        {"lat": lat - 1},
        {"lat": lat + 1},
        {"lon": lon - 1},
        {"lon": lon + 1},
    )
    opposite = (1, 0, 3, 2)

    def km_copy(side):
        return pltpu.make_async_remote_copy(
            src_ref=km,
            dst_ref=km_in.at[opposite[side]],
            send_sem=km_send.at[side],
            recv_sem=km_recv.at[opposite[side]],
            device_id=there[side],
            device_id_type=MESH,
        )

    def km_arrival(side):
        return pltpu.make_async_remote_copy(
            src_ref=km,
            dst_ref=km_in.at[side],
            send_sem=km_send.at[side],
            recv_sem=km_recv.at[side],
            device_id=there[side],
            device_id_type=MESH,
        )

    for side in range(4):

        @pl.when(has[side])
        def _():
            km_copy(side).start()

        @pl.when(jnp.logical_not(has[side]))
        def _():
            km_in[side] = jnp.zeros((2, rows, cols), jnp.float32)

    recv[me] = send[me]
    acc[...] = jnp.zeros(acc.shape, jnp.float32)
    group = a_ref.shape[1] // slots
    step_rows = math.gcd(rows, 4)

    @pl.loop(0, tiles // group)
    def _(chunk):
        pieces = []
        for i in range(group):
            k = chunk * group + i
            origin = lax.rem(me + tiles - k, tiles)

            @pl.when(k > 0)
            def _():
                item_copy(origin, origin).wait_recv()

            pieces.append(recv[origin])
        items = pieces[0] if group == 1 else jnp.concatenate(pieces, axis=1)
        depth = items.shape[1]
        val, fy, fx, fz = items[0:1], items[1:2], items[2:3], items[3:4]
        ch, row, col = items[4:5], items[5:6], items[6:7]
        a_ref[...] = hat(iota_f((chans, depth), 0), ch, val * (1.0 - fz), val * fz)
        b_ref[...] = hat(iota_f((rows, depth), 0), row, 1.0 - fy, fy)
        hi, lo = split2(hat(iota_f((cols, depth), 0), col, 1.0 - fx, fx))
        r_hi[...] = hi
        r_lo[...] = lo

        @pl.loop(0, rows // step_rows)
        def _(part):
            lefts = [
                a_ref[...] * b_ref[pl.ds(part * step_rows + j, 1), :] for j in range(step_rows)
            ]
            left_hi, left_lo = split2(jnp.concatenate(lefts, axis=0))
            dot = functools.partial(
                lax.dot_general, dimension_numbers=NT, preferred_element_type=jnp.float32
            )
            total = dot(left_hi, r_hi[...]) + dot(left_lo, r_hi[...]) + dot(left_hi, r_lo[...])
            here = pl.ds(pl.multiple_of(part * step_rows, step_rows), step_rows)
            acc[here] += total.reshape(step_rows, chans, cols)

    for side in range(4):

        @pl.when(has[side])
        def _():
            km_arrival(side).wait_recv()
            km_copy(side).wait_send()

    kc, mc = km[0], km[1]

    def beside(plane):
        mid = km[plane]
        south = jnp.concatenate([km_in[0, plane][rows - 1 :], mid[: rows - 1]], axis=0)
        north = jnp.concatenate([mid[1:], km_in[1, plane][:1]], axis=0)
        west = jnp.concatenate([km_in[2, plane][:, cols - 1 :], mid[:, : cols - 1]], axis=1)
        east = jnp.concatenate([mid[:, 1:], km_in[3, plane][:, :1]], axis=1)
        return (south, north, west, east)

    faces = [0.5 * (kc + kn) * mc * mn for kn, mn in zip(beside(0), beside(1))]
    inv = 1.0 / (1.0 + faces[0] + faces[1] + faces[2] + faces[3])
    for side in range(4):
        coef[side] = faces[side] * inv
    coef[4] = inv
    coef[5] = mc

    def halo(sweep, side, arriving):
        slot = opposite[side] if not arriving else side
        if side < 2:
            src = u.at[sweep, 1 if side == 0 else rows]
            dst = u.at[sweep, 0 if slot == 0 else rows + 1]
        else:
            src = edge_out.at[sweep, side - 2]
            dst = edge_in.at[sweep, slot - 2]
        return pltpu.make_async_remote_copy(
            src_ref=src,
            dst_ref=dst,
            send_sem=halo_send.at[sweep, side],
            recv_sem=halo_recv.at[sweep, slot],
            device_id=there[side],
            device_id_type=MESH,
        )

    def exchange(sweep):
        for j in range(2):
            edge_out[sweep, j] = jnp.transpose(packs[j])[:rows]
        for side in (2, 3, 0, 1):

            @pl.when(has[side])
            def _():
                halo(sweep, side, False).start()

        for side in range(4):

            @pl.when(jnp.logical_not(has[side]))
            def _():
                if side < 2:
                    u[sweep, 0 if side == 0 else rows + 1] = jnp.zeros((chans, cols), jnp.float32)
                else:
                    edge_in[sweep, side - 2] = jnp.zeros((rows, chans), jnp.float32)

            @pl.when(has[side])
            def _():
                halo(sweep, side, True).wait_recv()
                halo(sweep, side, False).wait_send()

        for j in range(2):
            filled = jnp.concatenate(
                [edge_in[sweep, j], jnp.zeros((LANES - rows, chans), jnp.float32)], axis=0
            )
            edge_t[j] = jnp.transpose(filled)

    for copy in sig_copies:
        copy.wait()
    bal_hi, bal_lo = split2(jnp.transpose(balance[...]))
    bal_twice = jnp.concatenate([bal_hi, bal_hi], axis=1)

    @pl.loop(0, rows // step_rows)
    def _(part):
        lines = [part * step_rows + j for j in range(step_rows)]
        scaled = []
        for r in lines:
            scale = jnp.concatenate(
                [sig[h, pl.ds(r, chans, stride=rows), :] for h in range(halves)], axis=1
            )
            scaled.append(acc[r] * coef[5, pl.ds(r, 1), :] * scale)
        hi, lo = split2(jnp.concatenate(scaled, axis=1))
        balanced = jnp.dot(
            bal_twice, jnp.concatenate([hi, lo], axis=0), preferred_element_type=jnp.float32
        ) + jnp.dot(bal_lo, hi, preferred_element_type=jnp.float32)
        for j, r in enumerate(lines):
            start = balanced[:, j * cols : (j + 1) * cols] * coef[4, pl.ds(r, 1), :]
            acc[r] = start
            u[0, r + 1] = start

    lane = lax.broadcasted_iota(jnp.int32, (BAND, LANES), 1)

    @pl.loop(0, chans // BAND)
    def _(band):
        here = pl.ds(pl.multiple_of(band * BAND, BAND), BAND)
        first = jnp.zeros((BAND, LANES), jnp.float32)
        last = jnp.zeros((BAND, LANES), jnp.float32)
        for r in range(rows):
            first = pack(lane, r, 0, first, acc[r, here, :LANES])
            last = pack(lane, r, LANES - 1, last, acc[r, here, cols - LANES :])
        packs[0, here] = first
        packs[1, here] = last

    for sweep in range(3):
        exchange(sweep)

        @pl.loop(0, chans // BAND)
        def _(band):
            here = pl.ds(pl.multiple_of(band * BAND, BAND), BAND)
            edges = (edge_t[0, here], edge_t[1, here])
            first = jnp.zeros((BAND, LANES), jnp.float32)
            last = jnp.zeros((BAND, LANES), jnp.float32)

            def line(r):
                return [u[sweep, r, here, h * LANES : (h + 1) * LANES] for h in range(halves)]

            south, mid = line(0), line(1)
            for r in range(rows):
                north = line(r + 2)
                up = [pltpu.roll(p, 1, 1) for p in mid]
                down = [pltpu.roll(p, LANES - 1, 1) for p in mid]
                before = turn(edges[0], -r)
                after = turn(edges[1], LANES - 1 - r)
                west = [jnp.where(lane == 0, q, p) for p, q in zip(up, [before] + up[:-1])]
                east = [
                    jnp.where(lane == LANES - 1, q, p) for p, q in zip(down, down[1:] + [after])
                ]
                totals = []
                for h in range(halves):
                    part = pl.ds(h * LANES, LANES)
                    total = acc[r, here, part] + coef[0, r : r + 1, part] * south[h]
                    total = total + coef[1, r : r + 1, part] * north[h]
                    total = total + coef[2, r : r + 1, part] * west[h]
                    total = total + coef[3, r : r + 1, part] * east[h]
                    totals.append(total)
                    if sweep < 2:
                        u[sweep + 1, r + 1, here, part] = total
                    else:
                        sig[h, pl.ds(band * BAND * rows + r, BAND, stride=rows), :] = total
                if sweep < 2:
                    first = pack(lane, r, 0, first, totals[0])
                    last = pack(lane, r, LANES - 1, last, totals[-1])
                south, mid = mid, north
            if sweep < 2:
                packs[0, here] = first
                packs[1, here] = last

    out_copies = [
        pltpu.make_async_copy(sig.at[h], out.at[:, pl.ds(h * LANES, LANES)], sig_sem.at[h])
        for h in range(halves)
    ]
    for copy in out_copies:
        copy.start()

    @pl.loop(1, tiles)
    def _(k):
        item_copy(lax.rem(me + k, tiles), me).wait_send()

    for copy in out_copies:
        copy.wait()


def on_device(
    innovation,
    fractions,
    owner,
    obs_row,
    obs_col,
    obs_field,
    obs_level,
    land_mask,
    kappa,
    sigma,
    balance,
):
    n_lon = lax.axis_size("lon")
    n_lat = lax.axis_size("lat")
    tiles = n_lon * n_lat
    obs = innovation.shape[0]
    slots = 2 * obs // tiles
    chans, rows, cols = sigma.shape
    halves = cols // LANES
    depth = min(1024, tiles * slots)
    line = lambda x: x.reshape(1, obs)
    vmem = pl.BlockSpec(memory_space=pltpu.VMEM)
    f32 = jnp.float32
    field = pl.pallas_call(
        functools.partial(kernel, n_lon, n_lat),
        out_shape=jax.ShapeDtypeStruct((chans * rows, cols), f32),
        in_specs=[vmem] * 10 + [pl.BlockSpec(memory_space=pl.ANY)],
        out_specs=pl.BlockSpec(memory_space=pl.ANY),
        scratch_shapes=[
            pltpu.VMEM((halves, chans * rows, LANES), f32),
            pltpu.VMEM((tiles, 8, slots), f32),
            pltpu.VMEM((tiles, 8, slots), f32),
            pltpu.VMEM((2, rows, cols), f32),
            pltpu.VMEM((4, 2, rows, cols), f32),
            pltpu.VMEM((6, rows, cols), f32),
            pltpu.VMEM((chans, depth), f32),
            pltpu.VMEM((rows, depth), f32),
            pltpu.VMEM((cols, depth), jnp.bfloat16),
            pltpu.VMEM((cols, depth), jnp.bfloat16),
            pltpu.VMEM((rows, chans, cols), f32),
            pltpu.VMEM((3, rows + 2, chans, cols), f32),
            pltpu.VMEM((3, 2, rows, chans), f32),
            pltpu.VMEM((3, 2, rows, chans), f32),
            pltpu.VMEM((2, chans, LANES), f32),
            pltpu.VMEM((2, chans, LANES), f32),
            pltpu.SemaphoreType.DMA((halves,)),
            pltpu.SemaphoreType.DMA((tiles,)),
            pltpu.SemaphoreType.DMA((tiles,)),
            pltpu.SemaphoreType.DMA((4,)),
            pltpu.SemaphoreType.DMA((4,)),
            pltpu.SemaphoreType.DMA((3, 4)),
            pltpu.SemaphoreType.DMA((3, 4)),
        ],
        compiler_params=pltpu.CompilerParams(
            collective_id=0, has_side_effects=True, vmem_limit_bytes=56 * 1024 * 1024
        ),
    )(
        line(innovation),
        fractions,
        line(owner),
        line(obs_row),
        line(obs_col),
        line(obs_field),
        line(obs_level),
        land_mask,
        kappa,
        balance,
        sigma.reshape(chans * rows, cols),
    )
    return field.reshape(chans, rows, cols)


def solution(mesh):
    spread = P(("member", "lon", "lat"))
    in_specs = (
        spread,
        P(None, ("member", "lon", "lat")),
        P(("member", "lon", "lat"), None),
        spread,
        spread,
        spread,
        spread,
        P("lat", "lon"),
        P("lat", "lon"),
        P(None, "lat", "lon"),
        P(),
    )
    out_specs = P("member", "lat", "lon")
    return jax.shard_map(
        on_device, mesh=mesh, in_specs=in_specs, out_specs=out_specs, check_vma=False
    )
```

```python
import functools
import math

import jax
import jax.numpy as jnp
from jax import lax
from jax.experimental import pallas as pl
from jax.experimental.pallas import tpu as pltpu
from jax.sharding import PartitionSpec as P

LEV = 32
MESH = pl.DeviceIdType.MESH
NT = (((1,), (1,)), ((), ()))
LANES = 128
BAND = 8
GROUPS = 2
F8 = jnp.float8_e4m3fn
LIFT = 512.0


def iota_f(shape, dim):
    return lax.broadcasted_iota(jnp.int32, shape, dim).astype(jnp.float32)


def hat(ids, low, first, second):
    return jnp.where(ids == low, first, 0.0) + jnp.where(ids == low + 1.0, second, 0.0)


def split2(x):
    hi = x.astype(jnp.bfloat16)
    return hi, (x - hi.astype(jnp.float32)).astype(jnp.bfloat16)


def turn(x, shift):
    shift = shift % LANES
    return pltpu.roll(x, shift, 1) if shift else x


def pack(lane, r, held, first, last):
    both = turn(jnp.where(lane == LANES - 1, last, first), 2 * r + 1)
    return jnp.where((lane == 2 * r) | (lane == 2 * r + 1), both, held)


def buckets(innov, frac, owner, orow, ocol, ofield, olev, tiles, slots):
    obs = innov.shape[1]
    blk = math.gcd(obs, 256)
    dest = owner[...]
    hot = jnp.where(lax.broadcasted_iota(jnp.int32, (tiles, obs), 0) == dest, 1.0, 0.0)
    before = jnp.where(iota_f((blk, blk), 0) < iota_f((blk, blk), 1), 1.0, 0.0).astype(jnp.bfloat16)
    carry = jnp.zeros((tiles, 1), jnp.float32)
    ranks = []
    for b in range(obs // blk):
        part = hot[:, b * blk : (b + 1) * blk]
        ahead = jnp.dot(part.astype(jnp.bfloat16), before, preferred_element_type=jnp.float32) + carry
        ranks.append(jnp.sum(ahead * part, axis=0, keepdims=True))
        carry = carry + jnp.sum(part, axis=1, keepdims=True)
    rank = jnp.concatenate(ranks, axis=1)
    slot_hot = jnp.where(iota_f((slots, obs), 0) == rank, 1.0, 0.0).astype(jnp.bfloat16)
    channel = ofield[...] * LEV + olev[...]
    ints = [channel.astype(jnp.float32), orow[...].astype(jnp.float32), ocol[...].astype(jnp.float32)]
    rest = jnp.concatenate(
        [innov[...], frac[...]] + ints + [jnp.zeros((1, obs), jnp.float32)], axis=0
    )
    mine = lax.broadcasted_iota(jnp.int32, (tiles, 8, obs), 0) == dest[None]
    placed = jnp.zeros((tiles * 8, slots), jnp.float32)
    for piece in range(3):
        top = rest.astype(jnp.bfloat16).astype(jnp.float32)
        rest = rest - top
        spread = jnp.where(mine, top[None], 0.0).reshape(tiles * 8, obs).astype(jnp.bfloat16)
        placed = placed + lax.dot_general(spread, slot_hot, NT, preferred_element_type=jnp.float32)
    return placed.reshape(tiles, 8, slots)


def kernel(
    n_lon,
    n_lat,
    innov,
    frac,
    owner,
    orow,
    ocol,
    ofield,
    olev,
    mask,
    kappa,
    balance,
    sigma,
    out,
    sig,
    send,
    recv,
    km,
    km_in,
    coef,
    a_ref,
    b_ref,
    r_hi,
    r_fix,
    acc,
    u,
    edge_out,
    edge_in,
    edge_t,
    packs,
    sig_sem,
    send_sem,
    recv_sem,
    km_send,
    km_recv,
    halo_send,
    halo_recv,
):
    tiles = n_lon * n_lat
    rows, cols = mask.shape
    chans = balance.shape[0]
    slots = recv.shape[2]
    halves = cols // LANES
    lon = lax.axis_index("lon")
    lat = lax.axis_index("lat")
    me = lon * n_lat + lat

    def where_is(tile):
        return {"lon": tile // n_lat, "lat": lax.rem(tile, n_lat)}

    sig_copies = [
        pltpu.make_async_copy(sigma.at[:, pl.ds(h * LANES, LANES)], sig.at[h], sig_sem.at[h])
        for h in range(halves)
    ]
    for copy in sig_copies:
        copy.start()
    barrier = pltpu.get_barrier_semaphore()

    @pl.loop(1, tiles)
    def _(k):
        pl.semaphore_signal(
            barrier, inc=1, device_id=where_is(lax.rem(me + k, tiles)), device_id_type=MESH
        )

    maskf = mask[...].astype(jnp.float32)
    km[0] = kappa[...] * maskf
    km[1] = maskf
    send[...] = buckets(innov, frac, owner, orow, ocol, ofield, olev, tiles, slots)
    pl.semaphore_wait(barrier, tiles - 1)

    def item_copy(target, origin):
        return pltpu.make_async_remote_copy(
            src_ref=send.at[target],
            dst_ref=recv.at[origin],
            send_sem=send_sem.at[target],
            recv_sem=recv_sem.at[origin],
            device_id=where_is(target),
            device_id_type=MESH,
        )

    @pl.loop(1, tiles)
    def _(k):
        item_copy(lax.rem(me + k, tiles), me).start()

    has = (lat > 0, lat < n_lat - 1, lon > 0, lon < n_lon - 1)
    there = (
        {"lat": lat - 1},
        {"lat": lat + 1},
        {"lon": lon - 1},
        {"lon": lon + 1},
    )
    opposite = (1, 0, 3, 2)

    def km_copy(side):
        return pltpu.make_async_remote_copy(
            src_ref=km,
            dst_ref=km_in.at[opposite[side]],
            send_sem=km_send.at[side],
            recv_sem=km_recv.at[opposite[side]],
            device_id=there[side],
            device_id_type=MESH,
        )

    def km_arrival(side):
        return pltpu.make_async_remote_copy(
            src_ref=km,
            dst_ref=km_in.at[side],
            send_sem=km_send.at[side],
            recv_sem=km_recv.at[side],
            device_id=there[side],
            device_id_type=MESH,
        )

    for side in range(4):

        @pl.when(has[side])
        def _():
            km_copy(side).start()

        @pl.when(jnp.logical_not(has[side]))
        def _():
            km_in[side] = jnp.zeros((2, rows, cols), jnp.float32)

    recv[me] = send[me]
    acc[...] = jnp.zeros(acc.shape, jnp.float32)
    group = a_ref.shape[1] // slots
    step_rows = math.gcd(rows, 4)

    @pl.loop(0, tiles // group)
    def _(chunk):
        pieces = []
        for i in range(group):
            k = chunk * group + i
            origin = lax.rem(me + tiles - k, tiles)

            @pl.when(k > 0)
            def _():
                item_copy(origin, origin).wait_recv()

            pieces.append(recv[origin])
        items = pieces[0] if group == 1 else jnp.concatenate(pieces, axis=1)
        depth = items.shape[1]
        val, fy, fx, fz = items[0:1], items[1:2], items[2:3], items[3:4]
        ch, row, col = items[4:5], items[5:6], items[6:7]
        a_ref[...] = hat(iota_f((chans, depth), 0), ch, val * (1.0 - fz), val * fz)
        b_ref[...] = hat(iota_f((rows, depth), 0), row, 1.0 - fy, fy)
        right = hat(iota_f((cols, depth), 0), col, 1.0 - fx, fx)
        hi = right.astype(jnp.bfloat16)
        r_hi[...] = hi
        r_fix[:, :depth] = right.astype(F8)
        r_fix[:, depth:] = ((right - hi.astype(jnp.float32)) * LIFT).astype(F8)

        @pl.loop(0, rows // step_rows)
        def _(part):
            lefts = [
                a_ref[...] * b_ref[pl.ds(part * step_rows + j, 1), :] for j in range(step_rows)
            ]
            left = jnp.concatenate(lefts, axis=0)
            left_hi = left.astype(jnp.bfloat16)
            left_lo = ((left - left_hi.astype(jnp.float32)) * LIFT).astype(F8)
            left_fix = jnp.concatenate([left_lo, left.astype(F8)], axis=1)
            dot = functools.partial(
                lax.dot_general, dimension_numbers=NT, preferred_element_type=jnp.float32
            )
            total = dot(left_hi, r_hi[...]) + dot(left_fix, r_fix[...]) * (1.0 / LIFT)
            here = pl.ds(pl.multiple_of(part * step_rows, step_rows), step_rows)
            acc[here] += total.reshape(step_rows, chans, cols)

    for side in range(4):

        @pl.when(has[side])
        def _():
            km_arrival(side).wait_recv()
            km_copy(side).wait_send()

    kc, mc = km[0], km[1]

    def beside(plane):
        mid = km[plane]
        south = jnp.concatenate([km_in[0, plane][rows - 1 :], mid[: rows - 1]], axis=0)
        north = jnp.concatenate([mid[1:], km_in[1, plane][:1]], axis=0)
        west = jnp.concatenate([km_in[2, plane][:, cols - 1 :], mid[:, : cols - 1]], axis=1)
        east = jnp.concatenate([mid[:, 1:], km_in[3, plane][:, :1]], axis=1)
        return (south, north, west, east)

    faces = [0.5 * (kc + kn) * mc * mn for kn, mn in zip(beside(0), beside(1))]
    inv = 1.0 / (1.0 + faces[0] + faces[1] + faces[2] + faces[3])
    for side in range(4):
        coef[side] = faces[side] * inv
    coef[4] = inv
    coef[5] = mc

    width = chans // GROUPS

    def halo(sweep, group, side, arriving):
        slot = opposite[side] if not arriving else side
        if side < 2:
            part = pl.ds(group * width, width)
            src = u.at[sweep, 1 if side == 0 else rows, part]
            dst = u.at[sweep, 0 if slot == 0 else rows + 1, part]
        else:
            src = edge_out.at[sweep, group]
            dst = edge_in.at[sweep, group, slot - 2]
        return pltpu.make_async_remote_copy(
            src_ref=src,
            dst_ref=dst,
            send_sem=halo_send.at[sweep, group, side],
            recv_sem=halo_recv.at[sweep, group, slot],
            device_id=there[side],
            device_id_type=MESH,
        )

    def give(sweep, group):
        part = pl.ds(group * width, width)
        edge_out[sweep, group] = jnp.transpose(packs[part])[: 2 * rows]
        for side in (2, 3, 0, 1):

            @pl.when(has[side])
            def _():
                halo(sweep, group, side, False).start()

            @pl.when(jnp.logical_not(has[side]))
            def _():
                if side < 2:
                    u[sweep, 0 if side == 0 else rows + 1, part] = jnp.zeros(
                        (width, cols), jnp.float32
                    )
                else:
                    edge_in[sweep, group, side - 2] = jnp.zeros((2 * rows, width), jnp.float32)

    def take(sweep, group):
        for side in range(4):

            @pl.when(has[side])
            def _():
                halo(sweep, group, side, True).wait_recv()

        odd = lax.broadcasted_iota(jnp.int32, (2 * rows, width), 0) % 2 == 1
        west = pltpu.roll(edge_in[sweep, group, 0], 1, 0)
        east = pltpu.roll(edge_in[sweep, group, 1], 2 * rows - 1, 0)
        filled = jnp.concatenate(
            [jnp.where(odd, west, east), jnp.zeros((LANES - 2 * rows, width), jnp.float32)], axis=0
        )
        edge_t[pl.ds(group * width, width)] = jnp.transpose(filled)

    for copy in sig_copies:
        copy.wait()
    bal_hi, bal_lo = split2(jnp.transpose(balance[...]))
    bal_twice = jnp.concatenate([bal_hi, bal_hi], axis=1)

    @pl.loop(0, rows // step_rows)
    def _(part):
        lines = [part * step_rows + j for j in range(step_rows)]
        scaled = []
        for r in lines:
            scale = jnp.concatenate(
                [sig[h, pl.ds(r, chans, stride=rows), :] for h in range(halves)], axis=1
            )
            scaled.append(acc[r] * coef[5, pl.ds(r, 1), :] * scale)
        hi, lo = split2(jnp.concatenate(scaled, axis=1))
        balanced = jnp.dot(
            bal_twice, jnp.concatenate([hi, lo], axis=0), preferred_element_type=jnp.float32
        ) + jnp.dot(bal_lo, hi, preferred_element_type=jnp.float32)
        for j, r in enumerate(lines):
            start = balanced[:, j * cols : (j + 1) * cols] * coef[4, pl.ds(r, 1), :]
            acc[r] = start
            u[0, r + 1] = start

    lane = lax.broadcasted_iota(jnp.int32, (BAND, LANES), 1)

    bands = width // BAND
    for group in range(GROUPS):

        @pl.loop(group * bands, (group + 1) * bands)
        def _(band):
            here = pl.ds(pl.multiple_of(band * BAND, BAND), BAND)
            held = jnp.zeros((BAND, LANES), jnp.float32)
            for r in range(rows):
                held = pack(lane, r, held, acc[r, here, :LANES], acc[r, here, cols - LANES :])
            packs[here] = held

        give(0, group)

    for sweep, group in [(sweep, group) for sweep in range(3) for group in range(GROUPS)]:
        take(sweep, group)

        @pl.loop(group * bands, (group + 1) * bands)
        def _(band):
            here = pl.ds(pl.multiple_of(band * BAND, BAND), BAND)
            edges = edge_t[here]
            held = jnp.zeros((BAND, LANES), jnp.float32)

            def line(r):
                return [u[sweep, r, here, h * LANES : (h + 1) * LANES] for h in range(halves)]

            south, mid = line(0), line(1)
            for r in range(rows):
                north = line(r + 2)
                up = [pltpu.roll(p, 1, 1) for p in mid]
                down = [pltpu.roll(p, LANES - 1, 1) for p in mid]
                outer = turn(edges, -(2 * r + 1))
                west = [jnp.where(lane == 0, q, p) for p, q in zip(up, [outer] + up[:-1])]
                east = [
                    jnp.where(lane == LANES - 1, q, p) for p, q in zip(down, down[1:] + [outer])
                ]
                totals = []
                for h in range(halves):
                    part = pl.ds(h * LANES, LANES)
                    total = acc[r, here, part] + coef[0, r : r + 1, part] * south[h]
                    total = total + coef[1, r : r + 1, part] * north[h]
                    total = total + coef[2, r : r + 1, part] * west[h]
                    total = total + coef[3, r : r + 1, part] * east[h]
                    totals.append(total)
                    if sweep < 2:
                        u[sweep + 1, r + 1, here, part] = total
                    else:
                        sig[h, pl.ds(band * BAND * rows + r, BAND, stride=rows), :] = total
                if sweep < 2:
                    held = pack(lane, r, held, totals[0], totals[-1])
                south, mid = mid, north
            if sweep < 2:
                packs[here] = held

        if sweep < 2:
            give(sweep + 1, group)

    out_copies = [
        pltpu.make_async_copy(sig.at[h], out.at[:, pl.ds(h * LANES, LANES)], sig_sem.at[h])
        for h in range(halves)
    ]
    for copy in out_copies:
        copy.start()

    @pl.loop(1, tiles)
    def _(k):
        item_copy(lax.rem(me + k, tiles), me).wait_send()

    for sweep, group, side in [
        (a, b, c) for a in range(3) for b in range(GROUPS) for c in range(4)
    ]:

        @pl.when(has[side])
        def _():
            halo(sweep, group, side, False).wait_send()

    for copy in out_copies:
        copy.wait()


def on_device(
    innovation,
    fractions,
    owner,
    obs_row,
    obs_col,
    obs_field,
    obs_level,
    land_mask,
    kappa,
    sigma,
    balance,
):
    n_lon = lax.axis_size("lon")
    n_lat = lax.axis_size("lat")
    tiles = n_lon * n_lat
    obs = innovation.shape[0]
    slots = 2 * obs // tiles
    chans, rows, cols = sigma.shape
    halves = cols // LANES
    depth = min(1024, tiles * slots)
    line = lambda x: x.reshape(1, obs)
    vmem = pl.BlockSpec(memory_space=pltpu.VMEM)
    f32 = jnp.float32
    field = pl.pallas_call(
        functools.partial(kernel, n_lon, n_lat),
        out_shape=jax.ShapeDtypeStruct((chans * rows, cols), f32),
        in_specs=[vmem] * 10 + [pl.BlockSpec(memory_space=pl.ANY)],
        out_specs=pl.BlockSpec(memory_space=pl.ANY),
        scratch_shapes=[
            pltpu.VMEM((halves, chans * rows, LANES), f32),
            pltpu.VMEM((tiles, 8, slots), f32),
            pltpu.VMEM((tiles, 8, slots), f32),
            pltpu.VMEM((2, rows, cols), f32),
            pltpu.VMEM((4, 2, rows, cols), f32),
            pltpu.VMEM((6, rows, cols), f32),
            pltpu.VMEM((chans, depth), f32),
            pltpu.VMEM((rows, depth), f32),
            pltpu.VMEM((cols, depth), jnp.bfloat16),
            pltpu.VMEM((cols, 2 * depth), F8),
            pltpu.VMEM((rows, chans, cols), f32),
            pltpu.VMEM((3, rows + 2, chans, cols), f32),
            pltpu.VMEM((3, GROUPS, 2 * rows, chans // GROUPS), f32),
            pltpu.VMEM((3, GROUPS, 2, 2 * rows, chans // GROUPS), f32),
            pltpu.VMEM((chans, LANES), f32),
            pltpu.VMEM((chans, LANES), f32),
            pltpu.SemaphoreType.DMA((halves,)),
            pltpu.SemaphoreType.DMA((tiles,)),
            pltpu.SemaphoreType.DMA((tiles,)),
            pltpu.SemaphoreType.DMA((4,)),
            pltpu.SemaphoreType.DMA((4,)),
            pltpu.SemaphoreType.DMA((3, GROUPS, 4)),
            pltpu.SemaphoreType.DMA((3, GROUPS, 4)),
        ],
        compiler_params=pltpu.CompilerParams(
            collective_id=0, has_side_effects=True, vmem_limit_bytes=56 * 1024 * 1024
        ),
    )(
        line(innovation),
        fractions,
        line(owner),
        line(obs_row),
        line(obs_col),
        line(obs_field),
        line(obs_level),
        land_mask,
        kappa,
        balance,
        sigma.reshape(chans * rows, cols),
    )
    return field.reshape(chans, rows, cols)


def solution(mesh):
    spread = P(("member", "lon", "lat"))
    in_specs = (
        spread,
        P(None, ("member", "lon", "lat")),
        P(("member", "lon", "lat"), None),
        spread,
        spread,
        spread,
        spread,
        P("lat", "lon"),
        P("lat", "lon"),
        P(None, "lat", "lon"),
        P(),
    )
    out_specs = P("member", "lat", "lon")
    return jax.shard_map(
        on_device, mesh=mesh, in_specs=in_specs, out_specs=out_specs, check_vma=False
    )
```

```python
import functools
import math

import jax
import jax.numpy as jnp
from jax import lax
from jax.experimental import pallas as pl
from jax.experimental.pallas import tpu as pltpu
from jax.sharding import PartitionSpec as P

LEV = 32
MESH = pl.DeviceIdType.MESH
NT = (((1,), (1,)), ((), ()))
LANES = 128
BAND = 8
GROUPS = 2
F8 = jnp.float8_e4m3fn
LIFT = 512.0


def iota_f(shape, dim):
    return lax.broadcasted_iota(jnp.int32, shape, dim).astype(jnp.float32)


def hat(ids, low, first, second):
    return jnp.where(ids == low, first, 0.0) + jnp.where(ids == low + 1.0, second, 0.0)


def split2(x):
    hi = x.astype(jnp.bfloat16)
    return hi, (x - hi.astype(jnp.float32)).astype(jnp.bfloat16)


def turn(x, shift):
    shift = shift % LANES
    return pltpu.roll(x, shift, 1) if shift else x


def pack(lane, r, held, first, last):
    both = turn(jnp.where(lane == LANES - 1, last, first), 2 * r + 1)
    return jnp.where((lane == 2 * r) | (lane == 2 * r + 1), both, held)


def buckets(innov, frac, owner, orow, ocol, ofield, olev, tiles, slots):
    obs = innov.shape[1]
    blk = math.gcd(obs, 256)
    dest = owner[...]
    hot = jnp.where(lax.broadcasted_iota(jnp.int32, (tiles, obs), 0) == dest, 1.0, 0.0)
    before = jnp.where(iota_f((blk, blk), 0) < iota_f((blk, blk), 1), 1.0, 0.0).astype(jnp.bfloat16)
    carry = jnp.zeros((tiles, 1), jnp.float32)
    ranks = []
    for b in range(obs // blk):
        part = hot[:, b * blk : (b + 1) * blk]
        ahead = jnp.dot(part.astype(jnp.bfloat16), before, preferred_element_type=jnp.float32) + carry
        ranks.append(jnp.sum(ahead * part, axis=0, keepdims=True))
        carry = carry + jnp.sum(part, axis=1, keepdims=True)
    rank = jnp.concatenate(ranks, axis=1)
    slot_hot = jnp.where(iota_f((slots, obs), 0) == rank, 1.0, 0.0).astype(jnp.bfloat16)
    channel = ofield[...] * LEV + olev[...]
    ints = [channel.astype(jnp.float32), orow[...].astype(jnp.float32), ocol[...].astype(jnp.float32)]
    rest = jnp.concatenate(
        [innov[...], frac[...]] + ints + [jnp.zeros((1, obs), jnp.float32)], axis=0
    )
    mine = lax.broadcasted_iota(jnp.int32, (tiles, 8, obs), 0) == dest[None]
    placed = jnp.zeros((tiles * 8, slots), jnp.float32)
    for piece in range(3):
        top = rest.astype(jnp.bfloat16).astype(jnp.float32)
        rest = rest - top
        spread = jnp.where(mine, top[None], 0.0).reshape(tiles * 8, obs).astype(jnp.bfloat16)
        placed = placed + lax.dot_general(spread, slot_hot, NT, preferred_element_type=jnp.float32)
    return placed.reshape(tiles, 8, slots)


def kernel(
    n_lon,
    n_lat,
    innov,
    frac,
    owner,
    orow,
    ocol,
    ofield,
    olev,
    mask,
    kappa,
    balance,
    sigma,
    out,
    sig,
    send,
    recv,
    km,
    km_in,
    coef,
    a_ref,
    b_ref,
    r_hi,
    r_fix,
    acc,
    u,
    edge_out,
    edge_in,
    edge_t,
    packs,
    sig_sem,
    send_sem,
    recv_sem,
    km_send,
    km_recv,
    halo_send,
    halo_recv,
):
    tiles = n_lon * n_lat
    rows, cols = mask.shape
    chans = balance.shape[0]
    slots = recv.shape[2]
    halves = cols // LANES
    lon = lax.axis_index("lon")
    lat = lax.axis_index("lat")
    me = lon * n_lat + lat

    def where_is(tile):
        return {"lon": tile // n_lat, "lat": lax.rem(tile, n_lat)}

    sig_copies = [
        pltpu.make_async_copy(sigma.at[:, pl.ds(h * LANES, LANES)], sig.at[h], sig_sem.at[h])
        for h in range(halves)
    ]
    for copy in sig_copies:
        copy.start()
    barrier = pltpu.get_barrier_semaphore()

    @pl.loop(1, tiles)
    def _(k):
        pl.semaphore_signal(
            barrier, inc=1, device_id=where_is(lax.rem(me + k, tiles)), device_id_type=MESH
        )

    maskf = mask[...].astype(jnp.float32)
    km[0] = kappa[...] * maskf
    km[1] = maskf
    send[...] = buckets(innov, frac, owner, orow, ocol, ofield, olev, tiles, slots)
    pl.semaphore_wait(barrier, tiles - 1)

    def item_copy(target, origin):
        return pltpu.make_async_remote_copy(
            src_ref=send.at[target],
            dst_ref=recv.at[origin],
            send_sem=send_sem.at[target],
            recv_sem=recv_sem.at[origin],
            device_id=where_is(target),
            device_id_type=MESH,
        )

    @pl.loop(1, tiles)
    def _(k):
        item_copy(lax.rem(me + k, tiles), me).start()

    has = (lat > 0, lat < n_lat - 1, lon > 0, lon < n_lon - 1)
    there = (
        {"lat": lat - 1},
        {"lat": lat + 1},
        {"lon": lon - 1},
        {"lon": lon + 1},
    )
    opposite = (1, 0, 3, 2)

    def km_copy(side):
        return pltpu.make_async_remote_copy(
            src_ref=km,
            dst_ref=km_in.at[opposite[side]],
            send_sem=km_send.at[side],
            recv_sem=km_recv.at[opposite[side]],
            device_id=there[side],
            device_id_type=MESH,
        )

    def km_arrival(side):
        return pltpu.make_async_remote_copy(
            src_ref=km,
            dst_ref=km_in.at[side],
            send_sem=km_send.at[side],
            recv_sem=km_recv.at[side],
            device_id=there[side],
            device_id_type=MESH,
        )

    for side in range(4):

        @pl.when(has[side])
        def _():
            km_copy(side).start()

        @pl.when(jnp.logical_not(has[side]))
        def _():
            km_in[side] = jnp.zeros((2, rows, cols), jnp.float32)

    recv[me] = send[me]
    acc[...] = jnp.zeros(acc.shape, jnp.float32)
    group = a_ref.shape[1] // slots
    step_rows = math.gcd(rows, 8)

    @pl.loop(0, tiles // group)
    def _(chunk):
        pieces = []
        for i in range(group):
            k = chunk * group + i
            origin = lax.rem(me + tiles - k, tiles)

            @pl.when(k > 0)
            def _():
                item_copy(origin, origin).wait_recv()

            pieces.append(recv[origin])
        items = pieces[0] if group == 1 else jnp.concatenate(pieces, axis=1)
        depth = items.shape[1]
        val, fy, fx, fz = items[0:1], items[1:2], items[2:3], items[3:4]
        ch, row, col = items[4:5], items[5:6], items[6:7]
        a_ref[...] = hat(iota_f((chans, depth), 0), ch, val * (1.0 - fz), val * fz)
        b_ref[...] = hat(iota_f((rows, depth), 0), row, 1.0 - fy, fy)
        right = hat(iota_f((cols, depth), 0), col, 1.0 - fx, fx)
        hi = right.astype(jnp.bfloat16)
        r_hi[...] = hi
        r_fix[:, :depth] = right.astype(F8)
        r_fix[:, depth:] = ((right - hi.astype(jnp.float32)) * LIFT).astype(F8)

        @pl.loop(0, rows // step_rows)
        def _(part):
            lefts = [
                a_ref[...] * b_ref[pl.ds(part * step_rows + j, 1), :] for j in range(step_rows)
            ]
            left = jnp.concatenate(lefts, axis=0)
            left_hi = left.astype(jnp.bfloat16)
            left_lo = ((left - left_hi.astype(jnp.float32)) * LIFT).astype(F8)
            left_fix = jnp.concatenate([left_lo, left.astype(F8)], axis=1)
            dot = functools.partial(
                lax.dot_general, dimension_numbers=NT, preferred_element_type=jnp.float32
            )
            total = dot(left_hi, r_hi[...]) + dot(left_fix, r_fix[...]) * (1.0 / LIFT)
            here = pl.ds(pl.multiple_of(part * step_rows, step_rows), step_rows)
            acc[here] += total.reshape(step_rows, chans, cols)

    for side in range(4):

        @pl.when(has[side])
        def _():
            km_arrival(side).wait_recv()
            km_copy(side).wait_send()

    kc, mc = km[0], km[1]

    def beside(plane):
        mid = km[plane]
        south = jnp.concatenate([km_in[0, plane][rows - 1 :], mid[: rows - 1]], axis=0)
        north = jnp.concatenate([mid[1:], km_in[1, plane][:1]], axis=0)
        west = jnp.concatenate([km_in[2, plane][:, cols - 1 :], mid[:, : cols - 1]], axis=1)
        east = jnp.concatenate([mid[:, 1:], km_in[3, plane][:, :1]], axis=1)
        return (south, north, west, east)

    faces = [0.5 * (kc + kn) * mc * mn for kn, mn in zip(beside(0), beside(1))]
    inv = 1.0 / (1.0 + faces[0] + faces[1] + faces[2] + faces[3])
    for side in range(4):
        coef[side] = faces[side] * inv
    coef[4] = inv
    coef[5] = mc

    width = chans // GROUPS

    def halo(sweep, group, side, arriving):
        slot = opposite[side] if not arriving else side
        if side < 2:
            part = pl.ds(group * width, width)
            src = u.at[sweep, 1 if side == 0 else rows, part]
            dst = u.at[sweep, 0 if slot == 0 else rows + 1, part]
        else:
            src = edge_out.at[sweep, group]
            dst = edge_in.at[sweep, group, slot - 2]
        return pltpu.make_async_remote_copy(
            src_ref=src,
            dst_ref=dst,
            send_sem=halo_send.at[sweep, group, side],
            recv_sem=halo_recv.at[sweep, group, slot],
            device_id=there[side],
            device_id_type=MESH,
        )

    def give(sweep, group):
        part = pl.ds(group * width, width)
        edge_out[sweep, group] = jnp.transpose(packs[part])[: 2 * rows]
        for side in (2, 3, 0, 1):

            @pl.when(has[side])
            def _():
                halo(sweep, group, side, False).start()

            @pl.when(jnp.logical_not(has[side]))
            def _():
                if side < 2:
                    u[sweep, 0 if side == 0 else rows + 1, part] = jnp.zeros(
                        (width, cols), jnp.float32
                    )
                else:
                    edge_in[sweep, group, side - 2] = jnp.zeros((2 * rows, width), jnp.float32)

    def take(sweep, group):
        for side in range(4):

            @pl.when(has[side])
            def _():
                halo(sweep, group, side, True).wait_recv()

        odd = lax.broadcasted_iota(jnp.int32, (2 * rows, width), 0) % 2 == 1
        west = pltpu.roll(edge_in[sweep, group, 0], 1, 0)
        east = pltpu.roll(edge_in[sweep, group, 1], 2 * rows - 1, 0)
        filled = jnp.concatenate(
            [jnp.where(odd, west, east), jnp.zeros((LANES - 2 * rows, width), jnp.float32)], axis=0
        )
        edge_t[pl.ds(group * width, width)] = jnp.transpose(filled)

    for copy in sig_copies:
        copy.wait()
    bal_hi, bal_lo = split2(jnp.transpose(balance[...]))
    bal_twice = jnp.concatenate([bal_hi, bal_hi], axis=1)

    @pl.loop(0, rows // step_rows)
    def _(part):
        lines = [part * step_rows + j for j in range(step_rows)]
        scaled = []
        for r in lines:
            scale = jnp.concatenate(
                [sig[h, pl.ds(r, chans, stride=rows), :] for h in range(halves)], axis=1
            )
            scaled.append(acc[r] * coef[5, pl.ds(r, 1), :] * scale)
        hi, lo = split2(jnp.concatenate(scaled, axis=1))
        balanced = jnp.dot(
            bal_twice, jnp.concatenate([hi, lo], axis=0), preferred_element_type=jnp.float32
        ) + jnp.dot(bal_lo, hi, preferred_element_type=jnp.float32)
        for j, r in enumerate(lines):
            start = balanced[:, j * cols : (j + 1) * cols] * coef[4, pl.ds(r, 1), :]
            acc[r] = start
            u[0, r + 1] = start

    lane = lax.broadcasted_iota(jnp.int32, (BAND, LANES), 1)

    bands = width // BAND
    for group in range(GROUPS):

        @pl.loop(group * bands, (group + 1) * bands)
        def _(band):
            here = pl.ds(pl.multiple_of(band * BAND, BAND), BAND)
            held = jnp.zeros((BAND, LANES), jnp.float32)
            for r in range(rows):
                held = pack(lane, r, held, acc[r, here, :LANES], acc[r, here, cols - LANES :])
            packs[here] = held

        give(0, group)

    for sweep, group in [(sweep, group) for sweep in range(3) for group in range(GROUPS)]:
        take(sweep, group)

        @pl.loop(group * bands, (group + 1) * bands)
        def _(band):
            here = pl.ds(pl.multiple_of(band * BAND, BAND), BAND)
            edges = edge_t[here]
            held = jnp.zeros((BAND, LANES), jnp.float32)

            def line(r):
                return [u[sweep, r, here, h * LANES : (h + 1) * LANES] for h in range(halves)]

            south, mid = line(0), line(1)
            for r in range(rows):
                north = line(r + 2)
                up = [pltpu.roll(p, 1, 1) for p in mid]
                down = [pltpu.roll(p, LANES - 1, 1) for p in mid]
                outer = turn(edges, -(2 * r + 1))
                west = [jnp.where(lane == 0, q, p) for p, q in zip(up, [outer] + up[:-1])]
                east = [
                    jnp.where(lane == LANES - 1, q, p) for p, q in zip(down, down[1:] + [outer])
                ]
                totals = []
                for h in range(halves):
                    part = pl.ds(h * LANES, LANES)
                    total = acc[r, here, part] + coef[0, r : r + 1, part] * south[h]
                    total = total + coef[1, r : r + 1, part] * north[h]
                    total = total + coef[2, r : r + 1, part] * west[h]
                    total = total + coef[3, r : r + 1, part] * east[h]
                    totals.append(total)
                    if sweep < 2:
                        u[sweep + 1, r + 1, here, part] = total
                    else:
                        sig[h, pl.ds(band * BAND * rows + r, BAND, stride=rows), :] = total
                if sweep < 2:
                    held = pack(lane, r, held, totals[0], totals[-1])
                south, mid = mid, north
            if sweep < 2:
                packs[here] = held

        if sweep < 2:
            give(sweep + 1, group)

    out_copies = [
        pltpu.make_async_copy(sig.at[h], out.at[:, pl.ds(h * LANES, LANES)], sig_sem.at[h])
        for h in range(halves)
    ]
    for copy in out_copies:
        copy.start()

    @pl.loop(1, tiles)
    def _(k):
        item_copy(lax.rem(me + k, tiles), me).wait_send()

    for sweep, group, side in [
        (a, b, c) for a in range(3) for b in range(GROUPS) for c in range(4)
    ]:

        @pl.when(has[side])
        def _():
            halo(sweep, group, side, False).wait_send()

    for copy in out_copies:
        copy.wait()


def on_device(
    innovation,
    fractions,
    owner,
    obs_row,
    obs_col,
    obs_field,
    obs_level,
    land_mask,
    kappa,
    sigma,
    balance,
):
    n_lon = lax.axis_size("lon")
    n_lat = lax.axis_size("lat")
    tiles = n_lon * n_lat
    obs = innovation.shape[0]
    slots = 2 * obs // tiles
    chans, rows, cols = sigma.shape
    halves = cols // LANES
    depth = min(1024, tiles * slots)
    line = lambda x: x.reshape(1, obs)
    vmem = pl.BlockSpec(memory_space=pltpu.VMEM)
    f32 = jnp.float32
    field = pl.pallas_call(
        functools.partial(kernel, n_lon, n_lat),
        out_shape=jax.ShapeDtypeStruct((chans * rows, cols), f32),
        in_specs=[vmem] * 10 + [pl.BlockSpec(memory_space=pl.ANY)],
        out_specs=pl.BlockSpec(memory_space=pl.ANY),
        scratch_shapes=[
            pltpu.VMEM((halves, chans * rows, LANES), f32),
            pltpu.VMEM((tiles, 8, slots), f32),
            pltpu.VMEM((tiles, 8, slots), f32),
            pltpu.VMEM((2, rows, cols), f32),
            pltpu.VMEM((4, 2, rows, cols), f32),
            pltpu.VMEM((6, rows, cols), f32),
            pltpu.VMEM((chans, depth), f32),
            pltpu.VMEM((rows, depth), f32),
            pltpu.VMEM((cols, depth), jnp.bfloat16),
            pltpu.VMEM((cols, 2 * depth), F8),
            pltpu.VMEM((rows, chans, cols), f32),
            pltpu.VMEM((3, rows + 2, chans, cols), f32),
            pltpu.VMEM((3, GROUPS, 2 * rows, chans // GROUPS), f32),
            pltpu.VMEM((3, GROUPS, 2, 2 * rows, chans // GROUPS), f32),
            pltpu.VMEM((chans, LANES), f32),
            pltpu.VMEM((chans, LANES), f32),
            pltpu.SemaphoreType.DMA((halves,)),
            pltpu.SemaphoreType.DMA((tiles,)),
            pltpu.SemaphoreType.DMA((tiles,)),
            pltpu.SemaphoreType.DMA((4,)),
            pltpu.SemaphoreType.DMA((4,)),
            pltpu.SemaphoreType.DMA((3, GROUPS, 4)),
            pltpu.SemaphoreType.DMA((3, GROUPS, 4)),
        ],
        compiler_params=pltpu.CompilerParams(
            collective_id=0, has_side_effects=True, vmem_limit_bytes=56 * 1024 * 1024
        ),
    )(
        line(innovation),
        fractions,
        line(owner),
        line(obs_row),
        line(obs_col),
        line(obs_field),
        line(obs_level),
        land_mask,
        kappa,
        balance,
        sigma.reshape(chans * rows, cols),
    )
    return field.reshape(chans, rows, cols)


def solution(mesh):
    spread = P(("member", "lon", "lat"))
    in_specs = (
        spread,
        P(None, ("member", "lon", "lat")),
        P(("member", "lon", "lat"), None),
        spread,
        spread,
        spread,
        spread,
        P("lat", "lon"),
        P("lat", "lon"),
        P(None, "lat", "lon"),
        P(),
    )
    out_specs = P("member", "lat", "lon")
    return jax.shard_map(
        on_device, mesh=mesh, in_specs=in_specs, out_specs=out_specs, check_vma=False
    )
```
